128 devices in a mesh: dp: 32 (over z, y, x_lo), branch: 4 (over x_hi, core).
Axes of the slice: x: 4 (x_hi: 2, x_lo: 2; x = x_hi * 2 + x_lo), y: 4, z: 4, core: 2. Of those that a mesh axis runs over, the one named last changes fastest.
Arguments:
- inputs: bfloat16 [16384, 2048], P('dp', 'branch'), may hold values from -6 to 6
- segment_ids: int32 [32, 512], P('dp'), may hold values from 0 to 5, never falling along the last dimension, each value on 1 to 256 neighbouring positions
- ln_gain: bfloat16 [2048], P('branch'), may hold values from 0.099609375 to 1.8984375
- ln_bias: bfloat16 [2048], P('branch'), may hold values from -3 to 3
- w_qkv: bfloat16 [2048, 3, 2048], P(None, None, 'branch'), may hold values from -0.125 to 0.125
- b_qkv: float32 [3, 2048], P(None, 'branch'), may hold values from -2.5 to 2.5
- w_out: bfloat16 [2048, 2048], P('branch'), may hold values from -0.375 to 0.375
- w_gate: bfloat16 [2048, 5632], P(None, 'branch'), may hold values from -0.125 to 0.125
- w_up: bfloat16 [2048, 5632], P(None, 'branch'), may hold values from -0.125 to 0.125
- w_down: bfloat16 [5632, 2048], P('branch'), may hold values from -0.078125 to 0.078125
- cotangent: bfloat16 [16384, 2048], P('dp', 'branch'), may hold values from -6 to 6
Outputs:
- output_rows: bfloat16 [16384, 2048], P('dp', 'branch')
- d_input: bfloat16 [16384, 2048], P('dp', 'branch')
- g_gain: float32 [2048], P('branch')
- g_bias: float32 [2048], P('branch')
- g_qkv: float32 [2048, 3, 2048], P('dp', None, 'branch')
- g_bqkv: float32 [3, 2048], P(None, 'branch')
- g_out: float32 [2048, 2048], P('branch', 'dp')
- g_gate: float32 [2048, 5632], P('dp', 'branch')
- g_up: float32 [2048, 5632], P('dp', 'branch')
- g_down: float32 [5632, 2048], P('branch', 'dp')
The draws below stay inside these ranges and needn't reach their ends.
Inputs may be any that keep to these rules, and one draw needn't show every extreme that they name: `segment_ids`: in each row the ids never fall, and each of the 6 documents has 1 to 256 tokens.
All inputs are finite; a program needn't handle non-finite values.
Results may differ from the reference program's by a relative error of at most 0.024.
Values may be sent and summed in bfloat16 or wider, within the bound.
No kernel may reach another device: no remote copies, remote signals or barrier semaphores. Data moves between devices by JAX's collectives and lax.ppermute only.
A program may use at most 192 MiB of HBM per device.

```python
import math
import jax
import jax.numpy as jnp
import numpy as np
from jax import lax

D = 2048
HEADS = 32
HD = 64
ROT = 16
FF = 5632
ROW_LEN = 512
DOCS = 6
E = 2048
TOKENS = 16384
N_DP = 32


def level_of(stream_key, shape, split, low, top_value):
    level, own = 1.0, jax.random.fold_in(stream_key, 6)
    for dim, shards_of in split:
        steps = jnp.exp(jax.random.uniform(jax.random.fold_in(own, dim), (shards_of,), jnp.float32, low / len(split), top_value / len(split)))
        level = level * jnp.repeat(steps, shape[dim] // shards_of).reshape([-1 if axis == dim else 1 for axis in range(len(shape))])
    return level


def split_up(count, total, limit, skew):
    loads = [(1 << 20) // math.isqrt(grade ** skew) + 1 for grade in range(2, count + 1)]
    rest, given = total - limit - (count - 1), [1] * (count - 1)
    while rest > 0:
        movable = [i for i in range(count - 1) if given[i] < limit]
        whole, budget = sum([loads[i] for i in movable]), rest
        for i in movable:
            addition = min(limit - given[i], max(1, budget * loads[i] // whole), rest)
            given[i] = given[i] + addition
            rest = rest - addition
    return np.array([limit] + given)


def uneven_parts(rng, amount, total, limit, skew):
    if amount == 2:
        one = jax.random.randint(rng, (), max(1, total - limit), min(limit, total - 1) + 1)
        return jnp.stack([one, total - one])
    tallies = jnp.asarray(split_up(amount, total, limit, skew), jnp.int32)
    pairs = (amount - 1) // 2
    donor, receiver = tallies[1:1 + 2 * pairs:2], tallies[2:2 + 2 * pairs:2]
    margin = jnp.minimum(donor - 1, limit - receiver)
    moved = jax.random.randint(jax.random.fold_in(rng, 1), (pairs,), 0, 1 << 20) % (margin + 1)
    tallies = tallies.at[1:1 + 2 * pairs:2].set(donor - moved).at[2:2 + 2 * pairs:2].set(receiver + moved)
    return tallies[jax.random.permutation(jax.random.fold_in(rng, 2), amount)]


def centred(rng, dims, spread, most, cuts=(), held_as=jnp.bfloat16):
    entries = spread * jax.random.normal(rng, dims, jnp.float32)
    if cuts:
        entries = entries * level_of(rng, dims, cuts, -0.22, 0.18)
    return jnp.clip(entries, -most, most).astype(held_as)


def setup_inputs(seed: int = 0) -> dict:
    splits = jax.random.split(jax.random.key(seed), 12)
    inputs = centred(splits[0], (TOKENS, D), 1.0, 6.0, ((0, 32), (1, 4)))
    segment_ids = jax.vmap(lambda own: jnp.searchsorted(jnp.cumsum(uneven_parts(own, DOCS, ROW_LEN, ROW_LEN // 2, 1)), jnp.arange(ROW_LEN), side="right"))(jax.random.split(splits[1], N_DP)).reshape((N_DP, ROW_LEN)).astype(jnp.int32)
    ln_gain = jnp.clip(1.0 + 0.18 * jax.random.normal(splits[2], (D,), jnp.float32), 0.099609375, 1.8984375).astype(jnp.bfloat16)
    ln_bias = centred(splits[3], (D,), 0.5, 3.0, ((0, 4),))
    w_qkv = centred(splits[4], (D, 3, E), D ** -0.5, 0.125, ((2, 4),))
    b_qkv = centred(splits[5], (3, E), 0.4, 2.5, ((1, 4),), jnp.float32)
    w_out = centred(splits[6], (E, D), (E // 8) ** -0.5, 0.375, ((0, 4),))
    w_gate = centred(splits[7], (D, FF), D ** -0.5, 0.125, ((1, 4),))
    w_up = centred(splits[8], (D, FF), D ** -0.5, 0.125, ((1, 4),))
    w_down = centred(splits[9], (FF, D), FF ** -0.5, 0.078125, ((0, 4),))
    cotangent = centred(splits[10], (TOKENS, D), 1.0, 6.0, ((0, 32), (1, 4)))
    return dict(inputs=inputs, segment_ids=segment_ids, ln_gain=ln_gain, ln_bias=ln_bias, w_qkv=w_qkv, b_qkv=b_qkv, w_out=w_out, w_gate=w_gate, w_up=w_up, w_down=w_down, cotangent=cotangent)


EPS = 1e-05
SCALE = 0.125
BIG = 1e+30
HIGH = lax.Precision.HIGHEST

@jax.custom_vjp
def low(v):
    return lax.optimization_barrier(v.astype(jnp.bfloat16)).astype(jnp.float32)

@jax.custom_vjp
def low_back(v):
    return v

def low_keep(v):
    return (low(v), None)

def low_pass(kept, grad):
    return (grad,)

def back_keep(v):
    return (v, None)

def back_low(kept, grad):
    return (low(grad),)
low.defvjp(low_keep, low_pass)
low_back.defvjp(back_keep, back_low)

def angle_tables(seg_row):
    length = seg_row.shape[0]
    index = jnp.arange(length, dtype=jnp.int32)
    change = jnp.concatenate([jnp.ones((1,), dtype=jnp.bool_), seg_row[1:] != seg_row[:-1]])
    starts = lax.cummax(jnp.where(change, index, jnp.zeros_like(index)), axis=0)
    position = (index - starts).astype(jnp.float32)
    freqs = 10000.0 ** (-2.0 * jnp.arange(ROT // 2, dtype=jnp.float32) / ROT)
    angles = position[:, None] * freqs[None, :]
    allowed = (index[None, :] <= index[:, None]) & (seg_row[None, :] == seg_row[:, None])
    return (jnp.cos(angles), jnp.sin(angles), allowed)

def rotate(tensor, cos_table, sin_table):
    halfway = ROT // 2
    lead_part = tensor[..., :halfway]
    tail_part = tensor[..., halfway:ROT]
    return jnp.concatenate([lead_part * cos_table - tail_part * sin_table, tail_part * cos_table + lead_part * sin_table, tensor[..., ROT:]], axis=-1)

def row_attention(args):
    query_r, key_r, value_r, allowed = args
    scores = jnp.einsum('qhd,khd->hqk', query_r, key_r, precision=HIGH) * SCALE
    scores = low_back(jnp.where(allowed[None], scores, -BIG))
    row_max = lax.optimization_barrier(jnp.max(scores, axis=-1, keepdims=True))
    weights = jnp.exp(scores - row_max)
    probs = low(weights / lax.optimization_barrier(jnp.sum(weights, axis=-1, keepdims=True)))
    return jnp.einsum('hqk,khd->qhd', probs, value_r, precision=HIGH)

def reference(inputs, segment_ids, ln_gain, ln_bias, w_qkv, b_qkv, w_out, w_gate, w_up, w_down, cotangent):
    cos_rows, sin_rows, allowed = jax.vmap(angle_tables)(segment_ids)
    cos_flat = cos_rows.reshape(TOKENS, 1, ROT // 2)
    sin_flat = sin_rows.reshape(TOKENS, 1, ROT // 2)

    def forward(x_float, gain, shift, wqkv, bqkv, wout, wgate, wup, wdown):
        row_mean = lax.optimization_barrier(jnp.mean(x_float, axis=-1, keepdims=True))
        centered = x_float - row_mean
        row_var = lax.optimization_barrier(jnp.mean(centered * centered, axis=-1, keepdims=True))
        normed = low(centered * lax.rsqrt(row_var + EPS) * gain + shift)
        proj = low_back(jnp.einsum('td,dce->tce', normed, wqkv, precision=HIGH) + bqkv)
        query_h = low(rotate(proj[:, 0].reshape(TOKENS, HEADS, HD), cos_flat, sin_flat))
        key_h = low(rotate(proj[:, 1].reshape(TOKENS, HEADS, HD), cos_flat, sin_flat))
        value_h = low(proj[:, 2].reshape(TOKENS, HEADS, HD))
        shape_rows = (N_DP, ROW_LEN, HEADS, HD)
        attended = lax.map(jax.checkpoint(row_attention), (query_h.reshape(shape_rows), key_h.reshape(shape_rows), value_h.reshape(shape_rows), allowed))
        attn_o = low(low_back(attended.reshape(TOKENS, E)))
        attn_out = jnp.dot(attn_o, wout, precision=HIGH)
        gate = low_back(jnp.dot(normed, wgate, precision=HIGH))
        up_proj = low_back(jnp.dot(normed, wup, precision=HIGH))
        activ = low(jax.nn.silu(gate) * up_proj)
        return x_float + attn_out + jnp.dot(activ, wdown, precision=HIGH)
    result, pull = jax.vjp(forward, inputs.astype(jnp.float32), ln_gain.astype(jnp.float32), ln_bias.astype(jnp.float32), w_qkv.astype(jnp.float32), b_qkv, w_out.astype(jnp.float32), w_gate.astype(jnp.float32), w_up.astype(jnp.float32), w_down.astype(jnp.float32))
    grads = pull(cotangent.astype(jnp.float32))
    return (result.astype(jnp.bfloat16), grads[0].astype(jnp.bfloat16), grads[1], grads[2], grads[3], grads[4], grads[5], grads[6], grads[7], grads[8])
```

```python
import functools

import jax
import jax.numpy as jnp
import numpy as np
from jax import lax
from jax.experimental import pallas as pl
from jax.experimental.pallas import tpu as pltpu
from jax.sharding import PartitionSpec as P

HD = 64
ROT = 16
EPS = 1e-05
SCALE = 0.125
BIG = 1e30

N_DP = 32
N_BR = 4
ROWS = 512
WIDTH = 2048
PART = 512
HIDDEN = 1408

BF = jnp.bfloat16
F32 = jnp.float32
VMEM_LIMIT = 67000000
VMEM_FULL = 66300000


def pair_up(axis, kind):
    pairs = []
    for d in range(N_DP):
        z, y, xl = (d // 8, d // 2 % 4, d % 2)
        if axis == "y":
            y = y ^ 1 if kind == "A" else 3 - y
        elif axis == "z":
            z = z ^ 1 if kind == "A" else 3 - z
        else:
            xl = 1 - xl
        pairs.append((d, z * 8 + y * 2 + xl))
    return pairs


def branch_pairs(mask):
    return [(b, b ^ mask) for b in range(N_BR)]


QUARTERS = (("y", "A"), ("y", "B"), ("z", "A"), ("z", "B"))
ORDER = {"A": (0, 3, 1, 2), "B": (0, 1, 2, 3)}


def block_order():
    table = []
    for axis, kind in QUARTERS:
        for first in ORDER[kind]:
            for second in ORDER[kind]:
                z, y = (second, first) if axis == "y" else (first, second)
                table.append(z * 4 + y)
    return np.array(table, np.int32)


def bits_of(position, kind):
    return (int(position in (1, 2)), position // 2) if kind == "A" else (position // 2, position % 2)


AT_BITS = 64
AT_XL = 80
AT_BRANCH = 81


def scalars():
    order = list(block_order())
    table = []
    for rank in range(N_DP):
        place = {"z": rank // 8, "y": rank // 2 % 4}
        bits = []
        for axis, kind in QUARTERS:
            other = "z" if axis == "y" else "y"
            bits += [*bits_of(place[axis], kind), *bits_of(place[other], kind)]
        table += [order + bits + [rank % 2, branch] for branch in range(N_BR)]
    table = jnp.asarray(np.array(table, np.int32))
    at = lax.axis_index("dp") * N_BR + lax.axis_index("branch")
    return lax.dynamic_index_in_dim(table, at, 0, keepdims=False)


def hop(array, quarter, step):
    axis, kind = QUARTERS[quarter]
    other = "z" if axis == "y" else "y"
    first, second = ("A", "B") if kind == "A" else ("B", "A")
    pairing = ((axis, first), (axis, second), (other, first), (other, second))[step]
    return lax.ppermute(array, "dp", pair_up(*pairing))


def shape(*dims, dtype=BF):
    return jax.ShapeDtypeStruct(dims, dtype)


ANY = pl.BlockSpec(memory_space=pltpu.HBM)
VMEM = pl.BlockSpec(memory_space=pltpu.VMEM)
SMEM = pl.BlockSpec(memory_space=pltpu.SMEM)
SMALL = pl.CostEstimate(flops=1000, bytes_accessed=1000, transcendentals=0)


class Loaded:
    def __init__(self, source, target, sem):
        self.target, self.copy = (target, pltpu.make_async_copy(source, target, sem))
        self.started, self.waited = (False, False)

    def start(self):
        if not self.started:
            self.copy.start()
            self.started = True

    def get(self):
        self.start()
        if not self.waited:
            self.copy.wait()
            self.waited = True
        return self.target


class Stored:
    def __init__(self, source, target, sem):
        self.ref, self.copy = (source, pltpu.make_async_copy(source, target, sem))
        self.started = False

    def flush(self):
        if not self.started:
            self.copy.start()
            self.started = True

    def get(self):
        return self.ref


class Sequence:
    def __init__(self, info):
        self.info = info
        self.token = None

    def __call__(self, name, body, outs, operands, hbm=(), scratch=(), lazy=0, here=(), full=False, stay=(), own=()):
        before = [] if self.token is None else [self.token]
        loads, raws, results, came = (len(operands), len(hbm), len(outs), len(here))

        def kernel(info, *refs):
            here_refs, refs = (refs[:came], refs[came:])
            sources, refs = (refs[:loads], refs[loads:])
            raw, refs = (refs[:raws], refs[raws + len(before) :])
            targets, refs = (refs[:results], refs[results:])
            stay_refs, refs = (refs[: len(stay)], refs[len(stay) :])
            own_refs, token, refs = (refs[: len(own)], refs[len(own)], refs[len(own) + 1 :])
            vmem_in, refs = (refs[:loads], refs[loads:])
            vmem_out, refs = (refs[:results], refs[results:])
            sems, rest = (refs[0], refs[1:])
            ins = [Loaded(a, b, sems.at[i]) for i, (a, b) in enumerate(zip(sources, vmem_in))]
            made = [Stored(a, b, sems.at[loads + i]) for i, (a, b) in enumerate(zip(vmem_out, targets))]
            token[...] = jnp.zeros(token.shape, token.dtype)
            for load in ins[: loads - lazy]:
                load.start()
            body(info, *ins, *here_refs, *raw, *made, *stay_refs, *own_refs, *(rest[:-1] if full else rest))
            for load in ins:
                load.get()
            for store in made:
                store.flush()
            for store in made:
                store.copy.wait()

        held = [pltpu.VMEM(a.shape, a.dtype) for a in (*operands, *outs)]
        scratch = list(scratch)
        if full:
            sized = [*held, *here, *[a for a in scratch if a.memory_space == pltpu.VMEM]]
            size = sum(int(np.prod(a.shape)) * jnp.dtype(a.dtype).itemsize for a in sized)
            scratch.append(pltpu.VMEM(((VMEM_FULL - size) // 4096 // 8 * 8, 1024), F32))
        results_ = pl.pallas_call(
            kernel,
            name=name,
            out_shape=[*outs, *stay, *own, shape(8, 128, dtype=F32)],
            in_specs=[SMEM] + [VMEM] * came + [ANY] * (loads + raws + len(before)),
            out_specs=[ANY] * results + [VMEM] * len(stay) + [ANY] * len(own) + [VMEM],
            scratch_shapes=[*held, pltpu.SemaphoreType.DMA((max(loads + results, 1),)), *scratch],
            compiler_params=pltpu.CompilerParams(vmem_limit_bytes=VMEM_LIMIT),
            cost_estimate=SMALL,
        )(self.info, *here, *operands, *hbm, *before)
        self.token = results_[-1]
        return results_[:-1]

    def pause(self, name, arrays, after=()):
        others = [*after] if self.token is None else [*after, self.token]
        count = len(arrays)

        def kernel(*refs):
            refs[-1][...] = jnp.zeros(refs[-1].shape, F32)

        results = pl.pallas_call(
            kernel,
            name=name,
            out_shape=[shape(*a.shape, dtype=a.dtype) for a in arrays] + [shape(8, 128, dtype=F32)],
            in_specs=[ANY] * count + [ANY] * len(others),
            out_specs=[ANY] * count + [VMEM],
            input_output_aliases={i: i for i in range(count)},
            compiler_params=pltpu.CompilerParams(vmem_limit_bytes=VMEM_LIMIT),
            cost_estimate=SMALL,
        )(*arrays, *others)
        self.token = results[-1]
        return results[:-1]


def dot(a, b):
    return jnp.dot(a, b, preferred_element_type=F32)


def dot_nt(a, b):
    return lax.dot_general(a, b, (((1,), (1,)), ((), ())), preferred_element_type=F32)


def dot_tn(a, b):
    return lax.dot_general(a, b, (((0,), (0,)), ((), ())), preferred_element_type=F32)


def span(index, size):
    return pl.ds(pl.multiple_of(index * size, size), size)


def copies(pairs, sems, start=True):
    made = []
    for i, (source, target) in enumerate(pairs):
        made.append(pltpu.make_async_copy(source, target, sems.at[i]))
        if start:
            made[-1].start()
    return made


def begin(waits):
    for wait in waits:
        wait.start()


FF_TILES = ((0, 512), (512, 512), (1024, 384))


def norm_body(info, x0, x1, x2, x3, gb0, gb1, gb2, gb3, normed, normed_t, stats, gain, *rest):
    sel, x_all, sems = (rest[:4], rest[4], rest[5])
    branch = info[AT_BRANCH]
    xs = [x0.get(), x1, x2, x3]
    places = [span(branch ^ mask, PART) for mask in range(4)]
    gbs = [gb[...] for gb in (gb0, gb1, gb2, gb3)]
    waits = copies([(x, x_all.at[:, place]) for place, x in zip(places, xs)], sems)
    for place, gb in zip(places, gbs):
        gain.ref[:, place] = jnp.broadcast_to(gb[0:1, :], (8, PART))

    def norm_rows(i, carry):
        at = span(i, 128)
        parts = [x[at, :].astype(F32) for x in xs]
        total = sum(jnp.sum(p, axis=1, keepdims=True) for p in parts)
        mean = total / WIDTH
        parts = [p - mean for p in parts]
        square = sum(jnp.sum(p * p, axis=1, keepdims=True) for p in parts)
        inv = lax.rsqrt(square / WIDTH + EPS)
        lane = lax.broadcasted_iota(jnp.int32, (128, 128), 1)
        stats.ref[at, :] = jnp.where(lane == 0, mean, inv)
        for place, p, gb in zip(places, parts, gbs):
            normed.ref[at, place] = (p * inv * gb[0:1, :] + gb[1:2, :]).astype(BF)
        return carry

    lax.fori_loop(0, 4, norm_rows, 0)
    for out in (normed, stats, gain):
        out.flush()
    for i in range(4):
        normed_t.ref[i * 512 : (i + 1) * 512, :] = normed.ref[:, i * 512 : (i + 1) * 512].T
    for quarter, out in enumerate(sel):
        s = info[AT_BITS + quarter * 4]
        gather(info, quarter, (1 - s) * 8, 8, normed_t.ref, out.ref)
        out.flush()
    normed_t.flush()
    for wait in waits:
        wait.wait()


def gather(info, quarter, start, count, left, lhs):
    for j in range(count):
        block = info[quarter * 16 + start + j]
        lhs[j * 128 : (j + 1) * 128, :] = left[span(block, 128), :]


def hidden_body(
    info, own, normed, by_core, by_high, by_both, w_down, w_gate, w_up, grad_t, activ, d_gu, *rest, pieces
):
    sends, (rows, d_act, wd, wg, wu, lhs, sems) = (rest[:4], rest[4:])
    moves = [(w_down.at[pl.ds(a, n)], wd.at[pl.ds(a, n)]) for a, n in FF_TILES]
    for a, n in FF_TILES:
        moves.append((w_gate.at[:, pl.ds(a, n)], wg.at[:, pl.ds(a, n)]))
        moves.append((w_up.at[:, pl.ds(a, n)], wu.at[:, pl.ds(a, n)]))
    waits = copies(moves, sems, start=False)
    begin(waits[:3])
    branch = info[AT_BRANCH]
    for mask, part in enumerate((own.get(), by_core, by_high, by_both)):
        place = span(branch ^ mask, PART)
        rows[:, place] = part[0:ROWS, :]
        grad_t.ref[place, :] = part[0:ROWS, :].T
    grad_t.flush()
    begin(waits[3:])
    for wait, (a, n) in zip(waits[:3], FF_TILES):
        wait.wait()
        d_act[:, a : a + n] = dot_nt(rows[...], wd[a : a + n, :])
    normed = normed.get()
    for wait in waits[3:]:
        wait.wait()
    for a, n in FF_TILES:
        at = slice(a, a + n)
        gate = dot(normed[...], wg[:, at])
        up = dot(normed[...], wu[:, at])
        sig = 0.5 + 0.5 * jnp.tanh(0.5 * gate)
        silu = gate * sig
        da = d_act[:, at]
        activ.ref[:, at] = (silu * up).astype(BF)
        d_gu.ref[:, at] = (da * up * sig * (1.0 + gate * (1.0 - sig))).astype(BF)
        d_gu.ref[:, HIDDEN + a : HIDDEN + a + n] = (da * silu).astype(BF)
    activ.flush()
    d_gu.flush()
    first_sends(info, pieces, grad_t.ref, activ.ref, d_gu.ref, sends, lhs)


def first_sends(info, pieces, grad_t, sum_right, token_right, sends, lhs):
    for quarter, ((a, b), (c, d)) in enumerate(pieces):
        send, base = (sends[quarter], (b - a) * 8)
        for j in range((d - c) // 128):
            columns = slice(c + j * 128, c + j * 128 + 128)
            send.ref[base + j * 512 : base + j * 512 + 512, :] = token_right[:, columns]
        s = info[AT_BITS + quarter * 4]
        gather(info, quarter, (1 - s) * 8, 8, grad_t, lhs)
        for i in (0, 512):
            sum_ = dot(lhs[i : i + 512, :], sum_right[:, a:b]).astype(BF)
            for j in range((b - a) // 128):
                send.ref[j * 1024 + i : j * 1024 + i + 512, :] = sum_[:, j * 128 : j * 128 + 128]
        send.flush()


def turn(t, cos, sin_up, sin_down, direction):
    ahead = pltpu.roll(t, 128 - ROT // 2, 1)
    behind = pltpu.roll(t, ROT // 2, 1)
    return t * cos[...] + direction * (ahead * sin_up[...] + behind * sin_down[...])


def attention_body(
    info, normed, b_qkv, cos, sin_up, sin_down, starts, grad_t, w_qkv, w_out, joined, g_bias, *rest, pieces, meanwhile
):
    sends, (wq, q, k, v, lhs, wo, d_attn, sems) = (rest[:4], rest[4:])
    waits = copies([*[(w_qkv.at[j], wq.at[j]) for j in range(3)], (w_out, wo)], sems)
    grad_t.start()
    g_bias.ref[...] = jnp.zeros(g_bias.ref.shape, F32)
    lane = lax.broadcasted_iota(jnp.int32, (1, 128), 1)
    left = normed.get()
    bias = b_qkv.get()
    tables = [t.get() for t in (cos, sin_up, sin_down)]
    starts = starts.get()
    for j, target in enumerate((q, k, v)):
        waits[j].wait()
        for a in range(0, PART, 256):
            t = dot(left[...], wq[j, :, a : a + 256]) + bias[j : j + 1, a : a + 256]
            for c in range(0, 256, 128):
                part = t[:, c : c + 128]
                if j < 2:
                    part = turn(part, *tables, 1.0)
                if j == 0:
                    part = part.astype(BF) * SCALE
                target[:, a + c : a + c + 128] = part.astype(BF)
    meanwhile()
    waits[3].wait()
    d_attn[...] = dot(wo[...], grad_t.get()[...]).astype(BF).T

    def pair_of_heads(i, carry):
        at = span(i, 128)
        dq, out = ([], [])
        dk = [jnp.zeros((256, 128), F32) for _ in range(2)]
        dv = [jnp.zeros((256, 128), F32) for _ in range(2)]
        first = lane < HD
        none = jnp.zeros((), BF)

        def both(t):
            return jnp.concatenate([jnp.where(first, t, none), jnp.where(first, none, t)], axis=0)

        for half in range(2):
            rows = slice(half * 256, half * 256 + 256)
            count = half * 256 + 256
            key_at = lax.broadcasted_iota(jnp.int32, (256, count), 1)
            row_at = lax.broadcasted_iota(jnp.int32, (256, count), 0) + half * 256
            allowed = (key_at <= row_at) & (key_at >= starts[rows, 0:1])
            allowed = jnp.concatenate([allowed, allowed], axis=0)
            q_h, do_h = (both(q[rows, at]), both(d_attn[rows, at]))
            keys = k[:count, at]
            values = v[:count, at]
            s = jnp.where(allowed, dot_nt(q_h, keys), -BIG)
            e = jnp.exp(s - jnp.max(s, axis=1, keepdims=True))
            p = e * (1.0 / jnp.sum(e, axis=1, keepdims=True))
            p_low = p.astype(BF)
            o = dot(p_low, values)
            out.append(jnp.where(first, o[:256], o[256:]))
            dp = dot_nt(do_h, values)
            ds = (p * (dp - jnp.sum(p * dp, axis=1, keepdims=True))).astype(BF)
            dq_h = dot(ds, keys) * SCALE
            dq.append(jnp.where(first, dq_h[:256], dq_h[256:]))
            dk_h = dot_tn(ds, q_h)
            dv_h = dot_tn(p_low, do_h)
            for part in range(half + 1):
                dk[part] = dk[part] + dk_h[part * 256 : part * 256 + 256]
                dv[part] = dv[part] + dv_h[part * 256 : part * 256 + 256]
        joined.ref[:, at] = jnp.concatenate(out, axis=0).astype(BF)
        dq, dk, dv = (jnp.concatenate(t, axis=0) for t in (dq, dk, dv))
        turned = [turn(t, *tables, -1.0) for t in (dq, dk)]
        for j, grad in enumerate((*turned, dv)):
            low = grad.astype(BF)
            joined.ref[:, pl.ds(pl.multiple_of((j + 1) * PART + i * 128, 128), 128)] = low
            g_bias.ref[j : j + 1, at] = jnp.sum(low.astype(F32), axis=0, keepdims=True)
        return carry

    lax.fori_loop(0, 4, pair_of_heads, 0)
    joined.flush()
    first_sends(info, pieces, grad_t.get(), joined.ref, joined.ref, sends, lhs)


def column_blocks(info):
    core = info[AT_BRANCH] % 2
    return [1 - core, 3 - core, core, 2 + core]


def output_loads(info, joined, activ, w_out, w_down, cat, w, sems):
    moves = [(joined.at[:, pl.ds(0, PART)], cat.at[:, pl.ds(0, PART)]), (activ, cat.at[:, pl.ds(PART, HIDDEN)])]
    for i, block in enumerate(column_blocks(info)):
        moves.append((w_out.at[:, span(block, PART)], w.at[i, pl.ds(0, PART)]))
        moves.append((w_down.at[:, span(block, PART)], w.at[i, pl.ds(PART, HIDDEN)]))
    return copies(moves, sems, start=False)


def output_body(send, keep, cat, w, waits):
    for wait in waits:
        wait.wait()
    for i in range(4):
        t = dot(cat[...], w[i])
        at = slice(i % 2 * ROWS, i % 2 * ROWS + ROWS)
        if i < 2:
            send.ref[at, :] = t.astype(BF)
        else:
            keep.ref[at, :] = t
        if i == 1:
            send.flush()


def two_parts(value):
    high = value.astype(BF).astype(F32)
    return (high, value - high)


def pack_sums(total, cross):
    row = lax.broadcasted_iota(jnp.int32, (16, ROWS), 0)
    packed = jnp.zeros((16, ROWS), F32)
    for i, part in enumerate((*two_parts(total), *two_parts(cross))):
        packed = jnp.where(row == i, part, packed)
    return packed.astype(BF)


def unpack_sums(packed):
    rows = packed.astype(F32)
    return (rows[0:1] + rows[1:2], rows[2:3] + rows[3:4])


def d_normed_loads(info, d_gu, w_qkv, w_gate, w_up, cat, w, sems):
    moves = [(d_gu, cat.at[:, pl.ds(3 * PART, 2 * HIDDEN)])]
    for i, block in enumerate(column_blocks(info)):
        place = span(block, PART)
        for j in range(3):
            moves.append((w_qkv.at[j, place], w.at[i, :, pl.ds(j * PART, PART)]))
        moves.append((w_gate.at[place], w.at[i, :, pl.ds(3 * PART, HIDDEN)]))
        moves.append((w_up.at[place], w.at[i, :, pl.ds(3 * PART + HIDDEN, HIDDEN)]))
    return copies(moves, sems, start=False)


def d_normed_body(info, joined, gain, x_all, stats, send, keep, sums, cat, w, waits):
    blocks = column_blocks(info)
    gain, x_all, stats = (t.get() for t in (gain, x_all, stats))
    cat[:, 0 : 3 * PART] = joined.ref[:, PART:]
    for wait in waits:
        wait.wait()
    mean = stats[:, 0:1]
    inv = stats[:, 1:2]
    total = jnp.zeros((ROWS, 1), F32)
    cross = jnp.zeros((ROWS, 1), F32)
    for i, block in enumerate(blocks):
        t = dot_nt(cat[...], w[i])
        place = span(block, PART)
        d_hat = t * gain[0:1, place]
        x_hat = (x_all[:, place].astype(F32) - mean) * inv
        total = total + jnp.sum(d_hat, axis=1, keepdims=True)
        cross = cross + jnp.sum(d_hat * x_hat, axis=1, keepdims=True)
        at = slice(i % 2 * ROWS, i % 2 * ROWS + ROWS)
        if i < 2:
            send.ref[at, :] = t.astype(BF)
        else:
            keep.ref[at, :] = t
    lane = lax.broadcasted_iota(jnp.int32, (ROWS, 128), 1)
    both = jnp.where(lane == 0, total, cross).T
    sums.ref[...] = both[0:8, :]
    send.ref[2 * ROWS : 2 * ROWS + 16, :] = pack_sums(both[0:1, :], both[1:2, :])


def chip_body(info, keep, got, send, mine):
    high = info[AT_BRANCH] // 2
    keep, got = (keep.get(), got.get())
    at, other = (span(high, ROWS), span(1 - high, ROWS))
    send.ref[0:ROWS, :] = (keep[other, :] + got[other, :].astype(F32)).astype(BF)
    mine.ref[...] = keep[at, :] + got[at, :].astype(F32)


def chip_sums_body(info, keep, sums, got, send, mine, chip_sums):
    chip_body(info, keep, got, send, mine)
    total, cross = unpack_sums(got.get()[2 * ROWS : 2 * ROWS + 16, :])
    sums = sums.get()
    total = total + sums[0:1, :]
    cross = cross + sums[1:2, :]
    row = lax.broadcasted_iota(jnp.int32, (8, ROWS), 0)
    chip_sums.ref[...] = jnp.where(row == 0, total, cross)
    send.ref[ROWS : ROWS + 16, :] = pack_sums(total, cross)


def nothing(info, *refs):
    pass


def small_body(info, lines, g_bqkv, g_gain, g_bias):
    small = jnp.sum(lines.get()[...].astype(F32), axis=0)
    rows = [jnp.concatenate([small[2 * i : 2 * i + 1], small[2 * i + 1 : 2 * i + 2]], axis=1) for i in range(5)]
    g_bqkv.ref[...] = jnp.concatenate(rows[:3], axis=0)
    g_gain.ref[...] = rows[3]
    g_bias.ref[...] = rows[4]


def rows_body(info, x, mine, got, out):
    out.ref[...] = (x.get()[...].astype(F32) + mine.get()[...] + got.get()[...].astype(F32)).astype(BF)


def d_input_body(info, x, cot, mine, stats, sums, g_bias, gain_bias, got, out, line):
    x, cot, mine, stats, sums, g_bias = (t.get() for t in (x, cot, mine, stats, sums, g_bias))
    own_gain = gain_bias.get()[0:1, :]
    total, cross = unpack_sums(got[ROWS : ROWS + 16, :])
    row = lax.broadcasted_iota(jnp.int32, (128, ROWS), 0)
    both = jnp.where(row == 0, total + sums[0:1, :], cross + sums[1:2, :]).T
    d_rows = mine[...] + got[0:ROWS, :].astype(F32)
    mean = stats[:, 0:1]
    inv = stats[:, 1:2]
    x_hat = (x[...].astype(F32) - mean) * inv
    d_hat = d_rows * own_gain
    back = inv * (d_hat - (both[:, 0:1] + x_hat * both[:, 1:2]) / WIDTH)
    out.ref[...] = (cot[...].astype(F32) + back).astype(BF)
    out.flush()
    rows = [g_bias[i : i + 1, :] for i in range(3)]
    rows += [jnp.sum(d_rows * x_hat, axis=0, keepdims=True), jnp.sum(d_rows, axis=0, keepdims=True)]
    rows = [row[:, a : a + 256] for row in rows for a in (0, 256)]
    one = jnp.concatenate([*rows, jnp.zeros((6, 256), F32)], axis=0).astype(BF)
    for i in range(N_DP):
        line.ref[i] = one


class Group:
    def __init__(self, sequence, name, pieces, rights, sends):
        self.sequence, self.name = (sequence, name)
        self.pieces, self.rights = (pieces, rights)
        self.sizes = [b - a + d - c for (a, b), (c, d) in pieces]
        self.sends, self.got, self.keep = (list(sends), [None] * 4, [None] * 4)

    def second(self, grad_t, normed_t, near, extra=None, outs=(), operands=(), raw=(), scratch=()):
        more = len(operands)

        def body(info, normed_t, *refs):
            near, got, (grad_t, sum_right), refs = (refs[:4], refs[4:8], refs[8:10], refs[10:])
            others, token_right, refs = (refs[:more], refs[more], refs[more + 1 :])
            raws, refs = (refs[: len(raw)], refs[len(raw) :])
            sends, keeps, refs = (refs[:4], refs[4:8], refs[8:])
            made, (lhs, wide, right, sems), rest = (
                refs[: len(outs)],
                refs[len(outs) : len(outs) + 4],
                refs[len(outs) + 4 :],
            )

            def own_columns(quarter):
                c, d = self.pieces[quarter][1]
                target = right.at[quarter % 2, pl.ds(0, ROWS), pl.ds(0, d - c)]
                return pltpu.make_async_copy(token_right.at[:, pl.ds(c, d - c)], target, sems.at[quarter])

            own = [own_columns(quarter) for quarter in range(4)]
            more_loads, finish = extra(info, others, raws, made, rest) if extra is not None else ([], None)
            for load in (normed_t, near[0], got[0], own[0], grad_t, sum_right):
                load.start()
            for quarter, ((a, b), (c, d)) in enumerate(self.pieces):
                n, base, slot = (b - a, (b - a) * 8, quarter % 2)
                if quarter < 3:
                    for load in (near[quarter + 1], got[quarter + 1], own[quarter + 1]):
                        load.start()
                if quarter == 1:
                    for load in (*others, *more_loads):
                        load.start()
                s = info[AT_BITS + quarter * 4]
                t = info[AT_BITS + quarter * 4 + 1]
                came, rows = (got[quarter].get(), near[quarter].get())
                for j in range((d - c) // 128):
                    block = came[base + j * 512 : base + j * 512 + 512, :]
                    right[slot, ROWS : 2 * ROWS, j * 128 : j * 128 + 128] = block
                own[quarter].wait()
                for out, side in ((sends[quarter], 1 - t), (keeps[quarter], t)):
                    start, part = (s * 8 + side * 4, span(side, 512))
                    for j in range(4):
                        block = info[quarter * 16 + start + j]
                        wide[j * 128 : (j + 1) * 128, 0:ROWS] = normed_t.get()[span(block, 128), :]
                    wide[:, ROWS : 2 * ROWS] = rows[part, :]
                    out.ref[:, n : n + d - c] = dot(wide[...], right[slot, :, 0 : d - c]).astype(BF)
                    gather(info, quarter, start, 4, grad_t.get(), lhs)
                    sum_ = dot(lhs[...], sum_right.get()[:, a:b])
                    for j in range(n // 128):
                        columns = slice(j * 128, j * 128 + 128)
                        block = came[span(2 * j + side, 512), :].astype(F32)
                        out.ref[:, columns] = (sum_[:, columns] + block).astype(BF)
                    out.flush()
            if finish is not None:
                finish()

        widest = max(d - c for _, (c, d) in self.pieces)
        results = self.sequence(
            self.name + "_second",
            body,
            [shape(512, n) for n in self.sizes] * 2 + list(outs),
            [normed_t, *near, *self.got, grad_t, self.rights[0], *operands],
            [self.rights[1], *raw],
            [
                pltpu.VMEM((512, ROWS), BF),
                pltpu.VMEM((512, 2 * ROWS), BF),
                pltpu.VMEM((2, 2 * ROWS, widest), BF),
                pltpu.SemaphoreType.DMA((4,)),
                *scratch,
            ],
            lazy=11 + more,
            full=True,
        )
        self.sends, self.keep = (list(results[:4]), list(results[4:8]))
        return results[8:]

    def go(self, step, after=(), extra=()):
        sends = self.sequence.pause(self.name + "_go" + str(step), [*self.sends, *extra], after=after)
        self.got = [hop(send, quarter, step) for quarter, send in enumerate(sends[:4])]
        return sends[4:]


class Tail:
    def __init__(self, sequence, groups, quarters):
        self.sequence, self.groups, self.quarters = (sequence, groups, quarters)
        self.early = False
        self.widths = [[group.sizes[quarter] for group in groups] for quarter in quarters]
        self.sizes = [sum(widths) for widths in self.widths]

    def ahead(self):
        n, group = (len(self.quarters), self.groups[0])

        def body(info, *refs):
            keep, got, sends, keeps = (refs[:n], refs[n : 2 * n], refs[2 * n : 3 * n], refs[3 * n :])
            for i, quarter in enumerate(self.quarters):
                bit = info[AT_BITS + quarter * 4 + 2]
                for out, side in ((sends[i], 1 - bit), (keeps[i], bit)):
                    at = span(side, 256)
                    out[...] = got[i].get()[at, :] + keep[i].get()[at, :]

        ins = [group.keep[quarter] for quarter in self.quarters] + [group.got[quarter] for quarter in self.quarters]
        sizes = [shape(256, widths[0]) for widths in self.widths]
        outs = self.sequence("ahead" + str(self.quarters[0]), body, [], ins, stay=sizes * 2)
        self.sends_ahead, self.keep_ahead, self.early = (outs[:n], outs[n:], True)

    def halve_first(self, after=(), extra=()):
        n = len(self.quarters)
        groups = self.groups[1:] if self.early else self.groups
        many, ready = (len(groups), [*self.sends_ahead] if self.early else [])

        def body(info, *refs):
            keep, got, refs = (refs[: n * many], refs[n * many : 2 * n * many], refs[2 * n * many :])
            ready_refs, refs = (refs[: len(ready)], refs[len(ready) :])
            keeps, sends, parts, sems = (
                refs[: n * many],
                refs[n * many : n * many + n],
                refs[n * many + n : 2 * n * many + n],
                refs[2 * n * many + n],
            )
            moves, places = ([], [])
            for i, widths in enumerate(self.widths):
                column = 0
                for j, width in enumerate(widths):
                    if self.early and j == 0:
                        moves.append((ready_refs[i], sends[i].at[:, pl.ds(0, width)]))
                    else:
                        one = i * many + j - (2 - many)
                        places.append((one, i, len(moves)))
                        moves.append((parts[one], sends[i].at[:, pl.ds(column, width)]))
                    column += width
            waits = copies(moves, sems, start=False)
            begin([waits[i] for i in range(len(moves)) if i not in [place[2] for place in places]])
            for one, i, move in places:
                bit = info[AT_BITS + self.quarters[i] * 4 + 2]
                for out, side in ((parts[one], 1 - bit), (keeps[one], bit)):
                    at = span(side, 256)
                    out[...] = got[one][at, :] + keep[one].get()[at, :]
                waits[move].start()
            for wait in waits:
                wait.wait()

        name = str(self.quarters[0])
        sizes = [shape(256, width) for widths in self.widths for width in widths[2 - many :]]
        outs = self.sequence(
            "halve2" + name,
            body,
            [],
            [group.keep[quarter] for quarter in self.quarters for group in groups],
            scratch=[*[pltpu.VMEM(a.shape, BF) for a in sizes], pltpu.SemaphoreType.DMA((2 * n,))],
            here=[*[group.got[quarter] for quarter in self.quarters for group in groups], *ready],
            stay=sizes,
            own=[shape(256, size) for size in self.sizes],
        )
        kept, outs = (outs[: n * many], outs[n * many :])
        sends = self.sequence.pause("go2" + name, [*outs, *extra], after=after) if after else outs
        self.got = [hop(send, quarter, 2) for quarter, send in zip(self.quarters, sends)]
        if self.early:
            self.keep = [list(pair) for pair in zip(self.keep_ahead, kept)]
        else:
            self.keep = [[kept[2 * i], kept[2 * i + 1]] for i in range(n)]
        return sends[n:]

    def halve_second(self):
        n = len(self.quarters)
        kept = [a for keep in self.keep for a in keep]

        def body(info, *refs):
            got, keep, sends, keeps = (refs[:n], refs[n : 3 * n], refs[3 * n : 4 * n], refs[4 * n :])
            for i, quarter in enumerate(self.quarters):
                bit = info[AT_BITS + quarter * 4 + 3]
                column = 0
                for part, width in zip(keep[2 * i : 2 * i + 2], self.widths[i]):
                    columns = slice(column, column + width)
                    for out, side in ((sends[i].ref, 1 - bit), (keeps[i], bit)):
                        at = span(side, 128)
                        out[:, columns] = got[i][at, columns] + part[at, :]
                    column += width
                sends[i].flush()

        sizes = [shape(128, size) for size in self.sizes]
        outs = self.sequence("halve3" + str(self.quarters[0]), body, sizes, [], here=[*self.got, *kept], stay=sizes)
        self.got = [hop(send, quarter, 3) for quarter, send in zip(self.quarters, outs[:n])]
        self.keep = outs[n:]

    def last(self):
        n = len(self.quarters)

        def body(info, *refs):
            got, keep, send, mine = (refs[:n], refs[n : 2 * n], refs[2 * n], refs[2 * n + 1])
            xl = info[AT_XL]
            column = 0
            for i, width in enumerate(self.sizes):
                for out, side in ((send.ref, 1 - xl), (mine, xl)):
                    at = span(side, 64)
                    out[:, column : column + width] = got[i][at, :] + keep[i][at, :]
                column += width

        one = [shape(64, sum(self.sizes))]
        send, mine = self.sequence("last" + str(self.quarters[0]), body, one, [], here=[*self.got, *self.keep], stay=one)
        return ([lax.ppermute(send, "dp", pair_up("x", ""))], [sum(self.sizes)], mine)

    def cross(self):
        n = len(self.quarters)
        kept = [a for keep in self.keep for a in keep]

        def body(info, *refs):
            got, keep, send, mine = (refs[:n], refs[n : 3 * n], refs[3 * n], refs[3 * n + 1])
            xl = info[AT_XL]
            start = 0
            for i in range(n):
                column = 0
                for part, width in zip(keep[2 * i : 2 * i + 2], self.widths[i]):
                    columns = slice(column, column + width)
                    for out, side in ((send.ref, 1 - xl), (mine, xl)):
                        for j in range(2):
                            at = span(2 * j + side, 64)
                            sum_ = got[i][at, columns] + part[at, :]
                            out[j * 64 : j * 64 + 64, start + column : start + column + width] = sum_
                    column += width
                start += column

        one = [shape(128, sum(self.sizes))]
        send, self.keep = self.sequence("cross" + str(self.quarters[0]), body, one, [], here=[*self.got, *kept], stay=one)
        self.got = lax.ppermute(send, "dp", pair_up("x", ""))

    def last_halving(self):
        n = len(self.quarters)

        def body(info, got, keep, *refs):
            sends, mine = (refs[:n], refs[n])
            column = 0
            for i, quarter in enumerate(self.quarters):
                bit = info[AT_BITS + quarter * 4 + 3]
                columns = slice(column, column + self.sizes[i])
                at = span(1 - bit, 64)
                sends[i].ref[...] = got[at, columns] + keep[at, columns]
                at = span(bit, 64)
                mine[:, columns] = got[at, columns] + keep[at, columns]
                column += self.sizes[i]

        outs = self.sequence(
            "last" + str(self.quarters[0]),
            body,
            [shape(64, size) for size in self.sizes],
            [],
            here=[self.got, self.keep],
            stay=[shape(64, sum(self.sizes))],
        )
        return ([hop(send, quarter, 3) for quarter, send in zip(self.quarters, outs)], self.sizes, outs[n])


def result(sequence, ends, outs, stacked):
    flat = len(outs)
    counts = [len(got) for got, _, _ in ends]

    def body(info, *refs):
        pieces, at = ([], 0)
        for (_, widths, _), count in zip(ends, counts):
            got, mine, refs = (refs[:count], refs[count], refs[count + 1 :])
            column = 0
            for one, width in zip(got, widths):
                pieces.append((at, at + width, one, mine, column))
                at, column = (at + width, column + width)
        for i, (_, places) in enumerate([*outs, *stacked]):
            for a, b, place in places:
                low, _, got, mine, column = [piece for piece in pieces if piece[0] <= place < piece[1]][0]
                here = place - low
                sum_ = got[:, here : here + b - a].astype(F32)
                sum_ = sum_ + mine[:, column + here : column + here + b - a].astype(F32)
                if i < flat:
                    refs[i].ref[:, a:b] = sum_
                else:
                    refs[flat].ref[i - flat, :, a:b] = sum_
            if i < flat:
                refs[i].flush()

    made = [shape(64, n, dtype=F32) for n, _ in outs] + [shape(len(stacked), 64, stacked[0][0], dtype=F32)]
    return sequence("result", body, made, [], here=[a for got, _, mine in ends for a in (*got, mine)])


def angle_tables(seg_row):
    length = seg_row.shape[0]
    index = jnp.arange(length, dtype=jnp.int32)
    change = jnp.concatenate([jnp.ones((1,), dtype=jnp.bool_), seg_row[1:] != seg_row[:-1]])
    starts = lax.cummax(jnp.where(change, index, jnp.zeros_like(index)), axis=0)
    position = (index - starts).astype(F32)
    freqs = 10000.0 ** (-2.0 * jnp.arange(ROT // 2, dtype=F32) / ROT)
    angles = position[:, None] * freqs[None, :]
    cos, sin = (jnp.cos(angles), jnp.sin(angles))
    half = ROT // 2
    ones = jnp.ones((length, HD - ROT), F32)
    none = jnp.zeros((length, half), F32)
    rest = jnp.zeros((length, HD - ROT), F32)
    cos_table = jnp.concatenate([cos, cos, ones] * 2, axis=1)
    up_table = jnp.concatenate([-sin, none, rest] * 2, axis=1)
    down_table = jnp.concatenate([none, sin, rest] * 2, axis=1)
    return (cos_table, up_table, down_table, jnp.broadcast_to(starts[:, None], (length, 128)))


DOWN_BLOCKS = (2, 3, 3, 3)
GU_BLOCKS = (7, 5, 5, 5)
OUT_BLOCKS = (1, 1, 1, 1)
QKV_BLOCKS = (3, 3, 3, 3)


def cut(blocks, offset=0):
    edges = [offset + 128 * sum(blocks[:i]) for i in range(5)]
    return list(zip(edges[:-1], edges[1:]))


def clip(places, low, high):
    kept = []
    for a, b, at in places:
        c, d = (max(a, low), min(b, high))
        if c < d:
            kept.append((c - low, d - low, at + c - a))
    return (high - low, kept)


def local(
    inputs, segment_ids, ln_gain, ln_bias, w_qkv, b_qkv, w_out, w_gate, w_up, w_down, cotangent
):
    run = Sequence(scalars())
    w_three = jnp.swapaxes(w_qkv, 0, 1)
    dma = pltpu.SemaphoreType.DMA
    tables = angle_tables(segment_ids[0])
    gb_own = jnp.stack([ln_gain, ln_bias]).astype(F32) + tables[3][0, 0].astype(F32)
    x_high = lax.ppermute(inputs, "branch", branch_pairs(2))
    x_core = lax.ppermute(inputs, "branch", branch_pairs(1))
    gb_far = [lax.ppermute(gb_own, "branch", branch_pairs(mask)) for mask in (1, 2, 3)]
    run.pause("prepare", [], after=[*tables, *gb_far])
    x_high, cot_own = run.pause("x_arrived", [x_high, cotangent])
    x_both = lax.ppermute(x_high, "branch", branch_pairs(1))
    cot_high = lax.ppermute(cot_own, "branch", branch_pairs(2))
    cot_core = lax.ppermute(cot_own, "branch", branch_pairs(1))
    cot_both = lax.ppermute(cot_high, "branch", branch_pairs(1))
    normed, normed_t, stats, gain, *sel, x_all = run(
        "norm",
        norm_body,
        [
            shape(ROWS, WIDTH),
            shape(WIDTH, ROWS),
            shape(ROWS, 128, dtype=F32),
            shape(8, WIDTH, dtype=F32),
            *[shape(1024, ROWS)] * 4,
        ],
        [inputs],
        scratch=[dma((4,))],
        here=[x_core, x_high, x_both, gb_own, *gb_far],
        own=[shape(ROWS, WIDTH)],
    )
    near = [hop(one, quarter, 0) for quarter, one in enumerate(sel)]
    hidden_pieces = list(zip(cut(DOWN_BLOCKS), cut(GU_BLOCKS)))
    head_pieces = list(zip(cut(OUT_BLOCKS), cut(QKV_BLOCKS, PART)))

    def first_shapes(pieces):
        return [shape((b - a) * 8 + (d - c) * 4, 128) for (a, b), (c, d) in pieces]

    grad_t, activ, d_gu, *sends = run(
        "hidden",
        functools.partial(hidden_body, pieces=hidden_pieces),
        [
            shape(WIDTH, ROWS),
            shape(ROWS, HIDDEN),
            shape(ROWS, 2 * HIDDEN),
            *first_shapes(hidden_pieces),
        ],
        [cotangent, normed],
        [w_down, w_gate, w_up],
        [
            pltpu.VMEM((ROWS, WIDTH), BF),
            pltpu.VMEM((ROWS, HIDDEN), F32),
            pltpu.VMEM((HIDDEN, WIDTH), BF),
            pltpu.VMEM((WIDTH, HIDDEN), BF),
            pltpu.VMEM((WIDTH, HIDDEN), BF),
            pltpu.VMEM((1024, ROWS), BF),
            dma((9,)),
        ],
        here=[cot_core, cot_high, cot_both],
        full=True,
    )
    hidden = Group(run, "hidden", hidden_pieces, [activ, d_gu], sends)
    hidden.go(0, after=near)
    def attention_d_normed(info, *refs):
        ins, (gain, x_all, stats), (d_gu, w_qkv, w_gate, w_up, w_out) = (refs[:7], refs[7:10], refs[10:15])
        joined, g_bias, sends, made, scratch = (refs[15], refs[16], refs[17:21], refs[21:24], refs[24:])
        cat, w, sems = scratch[8:]
        waits = d_normed_loads(info, d_gu, w_qkv, w_gate, w_up, cat, w, sems)

        def meanwhile():
            for load in (gain, x_all, stats):
                load.start()
            begin(waits)

        attention_body(
            info, *ins, w_qkv, w_out, joined, g_bias, *sends, *scratch[:8], pieces=head_pieces, meanwhile=meanwhile
        )
        d_normed_body(info, joined, gain, x_all, stats, *made, cat, w, waits)

    joined, g_bias, *sends, send_n, keep_n, sums = run(
        "attention_d_normed",
        attention_d_normed,
        [
            shape(ROWS, 4 * PART),
            shape(8, PART, dtype=F32),
            *first_shapes(head_pieces),
            shape(2 * ROWS + 16, PART),
            shape(2 * ROWS, PART, dtype=F32),
            shape(8, ROWS, dtype=F32),
        ],
        [normed, b_qkv, *tables, grad_t, gain, x_all, stats],
        [d_gu, w_three, w_gate, w_up, w_out],
        [
            pltpu.VMEM((3, WIDTH, PART), BF),
            *[pltpu.VMEM((ROWS, PART), BF)] * 3,
            pltpu.VMEM((1024, ROWS), BF),
            pltpu.VMEM((PART, WIDTH), BF),
            pltpu.VMEM((ROWS, PART), BF),
            dma((4,)),
            pltpu.VMEM((ROWS, 3 * PART + 2 * HIDDEN), BF),
            pltpu.VMEM((4, PART, 3 * PART + 2 * HIDDEN), BF),
            dma((21,)),
        ],
        lazy=4,
        full=True,
    )
    heads = Group(run, "heads", head_pieces, [joined, joined], sends)
    (send_n,) = heads.go(0, after=hidden.got, extra=[send_n])
    got_n = lax.ppermute(send_n, "branch", branch_pairs(1))
    hidden.second(grad_t, normed_t, near)
    hidden.go(1, after=[*heads.got, got_n])

    def chip_and_output(info, others, raws, made, scratch):
        cat, w, sems = scratch
        waits = output_loads(info, *raws, cat, w, sems)

        def finish():
            chip_sums_body(info, *others, *made[:3])
            for out in made[:3]:
                out.flush()
            output_body(*made[3:], cat, w, waits)

        return (waits, finish)

    send_n, mine_n, sums, send_o, keep_o = heads.second(
        grad_t,
        normed_t,
        near,
        chip_and_output,
        [
            shape(ROWS + 16, PART),
            shape(ROWS, PART, dtype=F32),
            shape(8, ROWS, dtype=F32),
            shape(2 * ROWS, PART),
            shape(2 * ROWS, PART, dtype=F32),
        ],
        [keep_n, sums, got_n],
        [joined, activ, w_out, w_down],
        [pltpu.VMEM((ROWS, PART + HIDDEN), BF), pltpu.VMEM((4, PART + HIDDEN, PART), BF), dma((10,))],
    )
    got_o = lax.ppermute(send_o, "branch", branch_pairs(1))
    (send_n,) = heads.go(1, after=hidden.got, extra=[send_n])
    got_n = lax.ppermute(send_n, "branch", branch_pairs(2))
    y_first = Tail(run, [hidden, heads], (0, 1))
    z_first = Tail(run, [hidden, heads], (2, 3))
    y_first.ahead()
    send_o, mine_o = run(
        "chip_output", chip_body, [shape(ROWS, PART), shape(ROWS, PART, dtype=F32)], [keep_o, got_o]
    )
    (send_o,) = y_first.halve_first(after=[*heads.got[2:], got_n], extra=[send_o])
    got_o = lax.ppermute(send_o, "branch", branch_pairs(2))
    z_first.halve_first()
    d_input, line = run(
        "d_input",
        d_input_body,
        [shape(ROWS, PART), shape(N_DP, 16, 256)],
        [inputs, cotangent, mine_n, stats, sums, g_bias, gb_own],
        here=[got_n],
    )
    lines = lax.all_to_all(line, "dp", 0, 0, tiled=True)
    y_first.cross()
    (lines,) = run.pause("lines_come", [lines], after=[got_o])
    z_first.halve_second()
    (output_rows,) = run("output_rows", rows_body, [shape(ROWS, PART)], [inputs, mine_o, got_o])
    z_end = z_first.last()
    ends = [y_first.last_halving(), z_end]
    g_bqkv, g_gain, g_bias = run(
        "small", small_body, [shape(n, PART, dtype=F32) for n in (3, 1, 1)], [lines]
    )
    down_at, gu_at, out_at, qkv_at, at = ([], [], [], [], 0)
    for pieces in zip(hidden_pieces, head_pieces):
        for (sums_, tokens), places in zip(pieces, ((down_at, gu_at), (out_at, qkv_at))):
            for (a, b), one in zip((sums_, tokens), places):
                one.append((a, b, at))
                at += b - a
    outs = [clip(down_at, 0, HIDDEN), clip(gu_at, 0, HIDDEN), clip(gu_at, HIDDEN, 2 * HIDDEN), clip(out_at, 0, PART)]
    stacked = [clip(qkv_at, PART * j, PART * (j + 1)) for j in (1, 2, 3)]
    g_down, g_gate, g_up, g_out, g_qkv = result(run, ends, outs, stacked)
    g_qkv = jnp.swapaxes(g_qkv, 0, 1)
    return (output_rows, d_input, g_gain[0], g_bias[0], g_qkv, g_bqkv, g_out.T, g_gate, g_up, g_down.T)


def solution(mesh):
    return jax.shard_map(
        local,
        mesh=mesh,
        in_specs=(
            P("dp", "branch"),
            P("dp", None),
            P("branch"),
            P("branch"),
            P(None, None, "branch"),
            P(None, "branch"),
            P("branch", None),
            P(None, "branch"),
            P(None, "branch"),
            P("branch", None),
            P("dp", "branch"),
        ),
        out_specs=(
            P("dp", "branch"),
            P("dp", "branch"),
            P("branch"),
            P("branch"),
            P("dp", None, "branch"),
            P(None, "branch"),
            P("branch", "dp"),
            P("dp", "branch"),
            P("dp", "branch"),
            P("branch", "dp"),
        ),
        check_vma=False,
    )
```
